32 devices in a mesh: slides: 1, row: 2 (over core), col: 16 (over z, y, x).
Axes of the slice: x: 2, y: 2, z: 4, core: 2. Of those that a mesh axis runs over, the one named last changes fastest.
Arguments:
- slide: bfloat16 [56, 112, 1024], P(('slides', 'row'), 'col'), may hold values from -6 to 6
- tissue: int32 [56, 112], P(('slides', 'row'), 'col'), may hold values from 0 to 1, as said below
- w_in: bfloat16 [1024, 2048], replicated, may hold values from -0.1875 to 0.1875
- w_bcd: bfloat16 [1024, 48], replicated, may hold values from -0.1875 to 0.1875
- dt_bias: float32 [16], replicated, may hold values from -2 to 1
- rate_x: float32 [16], replicated, as said below
- rate_y: float32 [16], replicated, as said below
- d_skip: float32 [16], replicated, may hold values from 0.5 to 2
- norm_gain: float32 [1024], replicated, may hold values from 0.1 to 1.9
- w_out: bfloat16 [1024, 1024], replicated, may hold values from -0.1875 to 0.1875
Outputs:
- mixed: bfloat16 [56, 112, 1024], P(('slides', 'row'), 'col')
The draws below stay inside these ranges and needn't reach their ends.
Inputs may be any that keep to these rules, and one draw needn't show every extreme that they name: 1 marks a tissue patch, 0 background. `rate_x`: positive decay rates per head. `rate_y`: positive decay rates per head.
All inputs are finite; a program needn't handle non-finite values.
Results may differ from the reference program's by a relative error of at most 0.013.
Values may be sent and summed in bfloat16 or wider, within the bound.
A program may use at most 320 MiB of HBM per device.

```python
import math
import jax
import jax.numpy as jnp
from jax import lax

D = 1024
HEADS = 16
HEAD_DIM = 64
STATE = 16
TILE_COLS = 7
INNER = 1024
ROWS = 56
COLS = 112


def draw_tissue(key, part):
    first_key, second_key = jax.random.split(key)
    tile_level = jax.random.randint(first_key, (COLS // TILE_COLS,), 0, 5)
    cell_draw = jax.random.randint(second_key, (ROWS, COLS), 0, 4)
    return (cell_draw < jnp.repeat(tile_level, TILE_COLS)[None, :]).astype(jnp.int32)


def draw_rate_x(key, part):
    picked = jax.random.uniform(jax.random.fold_in(key, 11), (HEADS,), jnp.float32)
    lower_end = jnp.log(0.2 / COLS)
    upper_end = jnp.log(1.0 / 24.0)
    return jnp.exp(lower_end + picked * (upper_end - lower_end)).astype(jnp.float32)


def draw_rate_y(key, part):
    picked = jax.random.uniform(jax.random.fold_in(key, 23), (HEADS,), jnp.float32)
    lower_end = jnp.log(0.2 / ROWS)
    upper_end = jnp.log(max(1.0 / 24.0, 4.0 / ROWS))
    return jnp.exp(lower_end + picked * (upper_end - lower_end)).astype(jnp.float32)


def block_levels(stream_key, shape, pieces, least, largest):
    loudness = 1.0
    for axis_at, blocks in pieces:
        heights = jax.random.uniform(jax.random.fold_in(jax.random.fold_in(stream_key, 6), axis_at), (blocks,), jnp.float32, least / len(pieces), largest / len(pieces))
        loudness = loudness * jnp.repeat(jnp.exp(heights), shape[axis_at] // blocks).reshape((-1,) + (1,) * (len(shape) - 1 - axis_at))
    return loudness


def centred(own_key, extent, width, reach, cuts=(), held_as=jnp.bfloat16):
    values = width * jax.random.normal(own_key, extent, jnp.float32)
    if cuts:
        values = values * block_levels(own_key, extent, cuts, -0.22, 0.18)
    return jnp.clip(values, -reach, reach).astype(held_as)


def setup_inputs(seed: int = 0, part: int = 0) -> dict:
    splits = jax.random.split(jax.random.key(seed), 11)
    own_keys = jax.random.split(jax.random.fold_in(splits[10], part), 11)
    slide = centred(own_keys[0], (ROWS, COLS, D), 1.0, 6.0, ((0, 2), (1, 16)))
    tissue = draw_tissue(jax.random.fold_in(jax.random.fold_in(splits[10], part), 71), part)
    w_in = centred(splits[2], (D, 2 * INNER), D ** -0.5, 0.1875)
    w_bcd = centred(splits[3], (D, 2 * STATE + HEADS), D ** -0.5, 0.1875)
    dt_bias = jnp.clip(jax.random.uniform(splits[4], (HEADS,), jnp.float32, -2.0, 1.0), -2.0, 1.0)
    rate_x = draw_rate_x(jax.random.fold_in(splits[10], 71), part)
    rate_y = draw_rate_y(jax.random.fold_in(splits[10], 71), part)
    d_skip = jnp.clip(jnp.exp(jax.random.uniform(splits[7], (HEADS,), jnp.float32, math.log(0.5), math.log(2.0))), 0.5, 2.0)
    norm_gain = jnp.clip(1.0 + 0.18 * jax.random.normal(splits[8], (INNER,), jnp.float32), 0.1, 1.9)
    w_out = centred(splits[9], (INNER, D), INNER ** -0.5, 0.1875)
    return dict(slide=slide, tissue=tissue, w_in=w_in, w_bcd=w_bcd, dt_bias=dt_bias, rate_x=rate_x, rate_y=rate_y, d_skip=d_skip, norm_gain=norm_gain, w_out=w_out)


def pair_chain(earlier, later):
    return (earlier[0] * later[0], later[0] * earlier[1] + later[1])

def reference(slide, tissue, w_in, w_bcd, dt_bias, rate_x, rate_y, d_skip, norm_gain, w_out):
    cell_mask = tissue.astype(jnp.float32).reshape(ROWS * COLS, 1)
    flat_cells = slide.reshape(ROWS * COLS, D)
    projected = jnp.dot(flat_cells, w_in, preferred_element_type=jnp.float32)
    values = projected[:, :INNER].astype(jnp.bfloat16) * cell_mask.astype(jnp.bfloat16)
    gate_z = projected[:, INNER:].astype(jnp.bfloat16)
    terms = jnp.dot(flat_cells, w_bcd, preferred_element_type=jnp.float32)
    b_map = terms[:, :STATE].astype(jnp.bfloat16).astype(jnp.float32).reshape(ROWS, COLS, STATE)
    c_map = terms[:, STATE:2 * STATE].astype(jnp.bfloat16).astype(jnp.float32).reshape(ROWS, COLS, STATE)
    step_sizes = (cell_mask * jax.nn.softplus(terms[:, 2 * STATE:] + dt_bias)).astype(jnp.bfloat16)
    step_sizes = step_sizes.astype(jnp.float32).reshape(ROWS, COLS, HEADS)
    channel_vals = values.astype(jnp.float32).reshape(ROWS, COLS, HEADS, HEAD_DIM)
    log_x = -step_sizes * rate_x
    log_y = -step_sizes * rate_y

    def row_step(carried, row_data):
        x_row, dt_row, b_row, c_row, lx_row, ly_row = row_data
        source = b_row[:, :, None, None] * (dt_row[..., None] * x_row)[:, None]
        decay = jnp.exp(lx_row)[:, None, :, None]
        scanned = lax.associative_scan(pair_chain, (decay, source), axis=0)
        state_row = jnp.exp(ly_row)[:, None, :, None] * carried + scanned[1]
        out_row = jnp.einsum('jn,jnhp->jhp', c_row, state_row, precision=lax.Precision.HIGHEST)
        out_row = out_row + d_skip[:, None] * x_row
        return (state_row, out_row)
    initial = jnp.zeros((COLS, STATE, HEADS, HEAD_DIM), jnp.float32)
    _, outputs = lax.scan(row_step, initial, (channel_vals, step_sizes, b_map, c_map, log_x, log_y))
    y_cells = outputs.reshape(ROWS * COLS, INNER).astype(jnp.bfloat16)
    gated = y_cells.astype(jnp.float32) * jax.nn.silu(gate_z.astype(jnp.float32))
    scaled = gated * lax.rsqrt(lax.optimization_barrier(jnp.mean(gated * gated, axis=-1, keepdims=True)) + 1e-05) * norm_gain
    result = jnp.dot(scaled.astype(jnp.bfloat16), w_out, preferred_element_type=jnp.float32) * cell_mask
    return result.astype(jnp.bfloat16).reshape(ROWS, COLS, D)
```

```python
import functools

import jax
import jax.numpy as jnp
from jax import lax
from jax.experimental import pallas as pl
from jax.experimental.pallas import tpu as pltpu
from jax.sharding import PartitionSpec as P

norm_eps = 1e-05
LANES = 128
SUB = 8
MESH = pl.DeviceIdType.MESH
f32, bf16 = jnp.float32, jnp.bfloat16


def kernel(dims, slide_ref, mask_ref, wbcd_ref, bias_ref, gain_ref, ratex_ref, ratey_ref, skip_ref,
           win_hbm, wout_hbm, out_ref,
           win, wout, send, recv, zs, tsc, lsc, ysc, state, carry, ysend, yrecv, yfull,
           w_sem, s_sem, r_sem, ys_sem, yr_sem, cs_sem, cr_sem, l_sem):
    n_row, n_col, rows, cols, inner, heads, width, n_state, block = dims
    ch = inner // n_col
    jp = n_col * SUB
    cells = rows * SUB
    blocks = ch // block
    me = lax.axis_index("col")
    my_row = lax.axis_index("row")
    head = lax.div(me * ch, width)
    dt_at = ch + 2 * n_state

    w1 = pltpu.make_async_copy(win_hbm.at[:, pl.ds(0, inner)], win.at[:, pl.ds(0, inner)], w_sem.at[0])
    w2 = pltpu.make_async_copy(win_hbm.at[:, pl.ds(inner, inner)], win.at[:, pl.ds(inner, inner)], w_sem.at[1])
    w3 = pltpu.make_async_copy(wout_hbm, wout, w_sem.at[2])
    w1.start()
    w2.start()
    w3.start()

    barrier = pltpu.get_barrier_semaphore()
    for o in range(1, n_col):
        pl.semaphore_signal(barrier, inc=1, device_id={"col": lax.rem(me + o, n_col)}, device_id_type=MESH)

    @pl.when(my_row > 0)
    def _():
        pl.semaphore_signal(barrier, inc=1, device_id={"row": my_row - 1}, device_id_type=MESH)

    @pl.when(my_row < n_row - 1)
    def _():
        pl.semaphore_signal(barrier, inc=1, device_id={"row": my_row + 1}, device_id_type=MESH)

    x = slide_ref[...]
    mask = mask_ref[...]
    lane = lax.broadcasted_iota(jnp.int32, (cells, LANES), 1)
    terms = jnp.dot(x, wbcd_ref[...], preferred_element_type=f32)
    biased = terms + bias_ref[...]
    steps = mask * (jnp.maximum(biased, 0.0) + jnp.log1p(jnp.exp(-jnp.abs(biased))))
    w1.wait()
    per = LANES // ch
    for t in range(inner // LANES):
        vals = jnp.dot(x, win[:, t * LANES:(t + 1) * LANES], preferred_element_type=f32)
        vals = vals.astype(bf16).astype(f32) * mask
        for q in range(per):
            d = t * per + q
            h = (d * ch) // width
            moved = vals if q == 0 else pltpu.roll(vals, LANES - q * ch, 1)
            dts = steps if h == 0 else pltpu.roll(steps, LANES - h, 1)
            chunk = jnp.where(lane < ch, moved, jnp.where(lane < dt_at, terms, dts))
            send[d] = chunk.astype(bf16)

    beside = jnp.where(my_row > 0, 1, 0) + jnp.where(my_row < n_row - 1, 1, 0)
    pl.semaphore_wait(barrier, n_col - 1 + beside)

    def forth(o):
        return pltpu.make_async_remote_copy(
            src_ref=send.at[lax.rem(me + o, n_col)], dst_ref=recv.at[me],
            send_sem=s_sem.at[o], recv_sem=r_sem.at[o],
            device_id={"col": lax.rem(me + o, n_col)}, device_id_type=MESH)

    for o in range(1, n_col):
        forth(o).start()
    own = pltpu.make_async_copy(send.at[me], recv.at[me], l_sem.at[0])
    own.start()

    w2.wait()
    for t in range(inner // LANES):
        zs[:, t * LANES:(t + 1) * LANES] = jnp.dot(
            x, win[:, inner + t * LANES:inner + (t + 1) * LANES], preferred_element_type=f32).astype(bf16)

    own.wait()
    for o in range(1, n_col):
        pltpu.make_async_remote_copy(
            src_ref=send.at[lax.rem(me + o, n_col)], dst_ref=recv.at[lax.rem(me + n_col - o, n_col)],
            send_sem=s_sem.at[o], recv_sem=r_sem.at[o],
            device_id={"col": lax.rem(me + o, n_col)}, device_id_type=MESH).wait()

    rate_x, rate_y, skip = ratex_ref[head], ratey_ref[head], skip_ref[head]
    down = lax.broadcasted_iota(jnp.int32, (jp, jp), 0)
    along = lax.broadcasted_iota(jnp.int32, (jp, jp), 1)
    tri = (along <= down).astype(bf16)
    cell_lane = lax.broadcasted_iota(jnp.int32, (jp, LANES), 1)

    def prepare(k, _):
        both = recv[:, pl.ds(pl.multiple_of(k * 16, 16), 16), :].astype(f32)
        for p in range(2):
            here = both[:, p * SUB:(p + 1) * SUB, :].reshape(jp, LANES)
            sums = jnp.dot(tri, here.astype(bf16), preferred_element_type=f32)
            sum_col = sums[:, dt_at:dt_at + 1]
            turned = jnp.where(cell_lane == dt_at + 1, sum_col, here).T
            tsc[2 * k + p] = turned
            gap = turned[dt_at + 1:dt_at + 2, :] - sum_col
            lsc[2 * k + p] = jnp.exp(jnp.where(down <= along, -rate_x * gap, -1e30)).astype(bf16)
        return 0

    lax.fori_loop(0, rows // 2, prepare, 0)

    def pass_down(cb):
        return pltpu.make_async_remote_copy(
            src_ref=state.at[cb], dst_ref=carry.at[cb],
            send_sem=cs_sem.at[cb], recv_sem=cr_sem.at[cb],
            device_id={"row": my_row + 1}, device_id_type=MESH)

    for cb in range(blocks):
        @pl.when(my_row == 0)
        def _():
            state[cb] = jnp.zeros_like(state[cb])

        @pl.when(my_row > 0)
        def _():
            pltpu.make_async_remote_copy(
                src_ref=state.at[cb], dst_ref=carry.at[cb],
                send_sem=cs_sem.at[cb], recv_sem=cr_sem.at[cb],
                device_id={"row": my_row - 1}, device_id_type=MESH).wait_recv()
            state[cb] = carry[cb]

        def one_row(i, _):
            v = tsc[i, cb * block:(cb + 1) * block, :]
            b = tsc[i, ch:ch + n_state, :]
            c = tsc[i, ch + n_state:ch + 2 * n_state, :]
            dt = tsc[i, dt_at:dt_at + 1, :]
            source = (b[:, None, :] * (v * dt)[None, :, :]).reshape(n_state * block, jp)
            hx = jnp.dot(source.astype(bf16), lsc[i], preferred_element_type=f32)
            now = jnp.exp(-rate_y * dt) * state[cb] + hx
            state[cb] = now
            y = jnp.sum(c[:, None, :] * now.reshape(n_state, block, jp), axis=0) + skip * v
            ysc[i, cb * block:(cb + 1) * block, :] = y
            return 0

        lax.fori_loop(0, rows, one_row, 0)

        @pl.when(my_row < n_row - 1)
        def _():
            pass_down(cb).start()

    def give_back(m, _):
        parts = []
        for g in range(2):
            pair = [ysc[4 * m + 2 * g], ysc[4 * m + 2 * g + 1]]
            if 2 * ch < LANES:
                pair.append(jnp.zeros((LANES - 2 * ch, jp), f32))
            parts.append(jnp.concatenate(pair, axis=0).T.reshape(n_col, SUB, LANES))
        ysend[:, pl.ds(pl.multiple_of(m * 16, 16), 16), :] = jnp.concatenate(parts, axis=1).astype(bf16)
        return 0

    lax.fori_loop(0, rows // 4, give_back, 0)

    def back(o):
        return pltpu.make_async_remote_copy(
            src_ref=ysend.at[lax.rem(me + o, n_col)], dst_ref=yrecv.at[me],
            send_sem=ys_sem.at[o], recv_sem=yr_sem.at[o],
            device_id={"col": lax.rem(me + o, n_col)}, device_id_type=MESH)

    for o in range(1, n_col):
        back(o).start()
    own_y = pltpu.make_async_copy(ysend.at[me], yrecv.at[me], l_sem.at[1])
    own_y.start()

    @pl.when(my_row < n_row - 1)
    def _():
        for cb in range(blocks):
            pass_down(cb).wait_send()

    w3.wait()
    own_y.wait()
    for o in range(1, n_col):
        pltpu.make_async_remote_copy(
            src_ref=ysend.at[lax.rem(me + o, n_col)], dst_ref=yrecv.at[lax.rem(me + n_col - o, n_col)],
            send_sem=ys_sem.at[o], recv_sem=yr_sem.at[o],
            device_id={"col": lax.rem(me + o, n_col)}, device_id_type=MESH).wait()

    half_lane = lax.broadcasted_iota(jnp.int32, (cells // 2, LANES), 1)
    squares = jnp.zeros((cells, 1), f32)
    for t in range(inner // LANES):
        parts = []
        for p in range(2):
            tile = None
            for q in range(per):
                piece = yrecv[t * per + q].astype(f32)
                shift = ((q - p) * ch) % LANES
                if shift:
                    piece = pltpu.roll(piece, shift, 1)
                tile = piece if tile is None else jnp.where(half_lane < q * ch, tile, piece)
            parts.append(tile.reshape(rows // 2, 1, SUB, LANES))
        y = jnp.concatenate(parts, axis=1).reshape(cells, LANES)
        z = zs[:, t * LANES:(t + 1) * LANES].astype(f32)
        g = y * (z * jax.nn.sigmoid(z))
        squares = squares + jnp.sum(g * g, axis=1, keepdims=True)
        yfull[:, t * LANES:(t + 1) * LANES] = g
    scale = lax.rsqrt(squares / inner + norm_eps)
    normed = (yfull[...] * scale * gain_ref[...]).astype(bf16)
    mixed = jnp.dot(normed, wout[...], preferred_element_type=f32) * mask
    out_ref[...] = mixed.reshape(rows, SUB, mixed.shape[1])[:, :cols, :].astype(bf16)


def per_device(slide, tissue, w_in, w_bcd, dt_bias, rate_x, rate_y, d_skip, norm_gain, w_out):
    rows, cols, model = slide.shape
    inner, heads = w_out.shape[0], dt_bias.shape[0]
    n_state = (w_bcd.shape[1] - heads) // 2
    width = inner // heads
    n_col, n_row = lax.axis_size("col"), lax.axis_size("row")
    ch = inner // n_col
    block = min(ch, 16)
    jp, cells = n_col * SUB, rows * SUB
    assert cols <= SUB and rows % 4 == 0 and 2 * ch <= LANES and width % ch == 0
    assert ch + 2 * n_state + heads <= LANES and ch % block == 0
    pad = SUB - cols
    x = jnp.pad(slide, ((0, 0), (0, pad), (0, 0))).reshape(cells, model)
    mask = jnp.pad(tissue.astype(f32), ((0, 0), (0, pad))).reshape(cells, 1)
    room = LANES - ch - w_bcd.shape[1]
    wbcd = jnp.pad(w_bcd, ((0, 0), (ch, room)))
    bias = jnp.pad(dt_bias, (ch + 2 * n_state, room)).reshape(1, LANES)
    vmem = pl.BlockSpec(memory_space=pltpu.VMEM)
    smem = pl.BlockSpec(memory_space=pltpu.SMEM)
    hbm = pl.BlockSpec(memory_space=pl.ANY)
    blocks = ch // block
    dims = (n_row, n_col, rows, cols, inner, heads, width, n_state, block)
    dma = pltpu.SemaphoreType.DMA
    return pl.pallas_call(
        functools.partial(kernel, dims),
        out_shape=jax.ShapeDtypeStruct((rows, cols, model), bf16),
        in_specs=[vmem] * 5 + [smem] * 3 + [hbm] * 2,
        out_specs=vmem,
        scratch_shapes=[
            pltpu.VMEM(w_in.shape, bf16),
            pltpu.VMEM(w_out.shape, bf16),
            pltpu.VMEM((n_col, cells, LANES), bf16),
            pltpu.VMEM((n_col, cells, LANES), bf16),
            pltpu.VMEM((cells, inner), bf16),
            pltpu.VMEM((rows, LANES, jp), f32),
            pltpu.VMEM((rows, jp, jp), bf16),
            pltpu.VMEM((rows, ch, jp), f32),
            pltpu.VMEM((blocks, n_state * block, jp), f32),
            pltpu.VMEM((blocks, n_state * block, jp), f32),
            pltpu.VMEM((n_col, cells // 2, LANES), bf16),
            pltpu.VMEM((n_col, cells // 2, LANES), bf16),
            pltpu.VMEM((cells, inner), f32),
            dma((3,)), dma((n_col,)), dma((n_col,)), dma((n_col,)), dma((n_col,)),
            dma((blocks,)), dma((blocks,)), dma((2,)),
        ],
        compiler_params=pltpu.CompilerParams(
            collective_id=0, has_side_effects=True, vmem_limit_bytes=60 * 1024 * 1024),
        cost_estimate=pl.CostEstimate(flops=4 * 10**9, bytes_accessed=8 * 10**6, transcendentals=10**6),
    )(x, mask, wbcd, bias, norm_gain.reshape(1, inner), rate_x, rate_y, d_skip, w_in, w_out)


def solution(mesh):
    grid = P(("slides", "row"), "col")
    return jax.shard_map(
        per_device,
        mesh=mesh,
        in_specs=(P(("slides", "row"), "col", None), grid) + (P(),) * 8,
        out_specs=P(("slides", "row"), "col", None),
        check_vma=False,
    )
```

```python
import functools

import jax
import jax.numpy as jnp
from jax import lax
from jax.experimental import pallas as pl
from jax.experimental.pallas import tpu as pltpu
from jax.sharding import PartitionSpec as P

norm_eps = 1e-05
LANES = 128
SUB = 8
MESH = pl.DeviceIdType.MESH
f32, bf16 = jnp.float32, jnp.bfloat16


def kernel(dims, slide_ref, tissue_ref, wbcd_ref, gain_ref, bias_ref, ratex_ref, ratey_ref, skip_ref,
           win_hbm, wout_hbm, out_ref,
           win, wout, send, recv, zs, tsc, fade, ysc, state, carry, ysend, yrecv, yfull,
           w_sem, s_sem, r_sem, ys_sem, yr_sem, cs_sem, cr_sem, l_sem):
    n_row, n_col, rows, cols, inner, heads, width, n_state, block, groups = dims
    ch = inner // n_col
    jp = n_col * SUB
    cells = rows * SUB
    blocks = ch // block
    me = lax.axis_index("col")
    my_row = lax.axis_index("row")
    head = lax.div(me * ch, width)
    dt_at = ch + 2 * n_state

    w1 = pltpu.make_async_copy(win_hbm.at[:, pl.ds(0, inner)], win.at[:, pl.ds(0, inner)], w_sem.at[0])
    w2 = pltpu.make_async_copy(win_hbm.at[:, pl.ds(inner, inner)], win.at[:, pl.ds(inner, inner)], w_sem.at[1])
    w3 = pltpu.make_async_copy(wout_hbm, wout, w_sem.at[2])
    w1.start()
    w2.start()
    w3.start()

    barrier = pltpu.get_barrier_semaphore()
    for o in range(1, n_col):
        pl.semaphore_signal(barrier, inc=1, device_id={"col": lax.rem(me + o, n_col)}, device_id_type=MESH)

    @pl.when(my_row > 0)
    def _():
        pl.semaphore_signal(barrier, inc=1, device_id={"row": my_row - 1}, device_id_type=MESH)

    @pl.when(my_row < n_row - 1)
    def _():
        pl.semaphore_signal(barrier, inc=1, device_id={"row": my_row + 1}, device_id_type=MESH)

    gap = jnp.zeros((rows, SUB - cols, slide_ref.shape[2]), f32)
    x = jnp.concatenate([slide_ref[...].astype(f32), gap], axis=1).reshape(cells, -1).astype(bf16)
    marks = jnp.concatenate([tissue_ref[...].astype(f32), jnp.zeros((SUB - cols, rows), f32)], axis=0)
    marks = jnp.concatenate([marks, jnp.zeros((SUB, LANES - rows), f32)], axis=1).T[:rows, :]
    spread = jnp.broadcast_to(marks[:, None, :], (rows, SUB, SUB))
    same = (lax.broadcasted_iota(jnp.int32, (rows, SUB, SUB), 1)
            == lax.broadcasted_iota(jnp.int32, (rows, SUB, SUB), 2))
    mask = jnp.sum(jnp.where(same, spread, 0.0), axis=2, keepdims=True).reshape(cells, 1)
    lane = lax.broadcasted_iota(jnp.int32, (cells, LANES), 1)
    terms = lax.dot_general(x, wbcd_ref[...], (((1,), (1,)), ((), ())), preferred_element_type=f32)
    terms = jnp.concatenate(
        [jnp.zeros((cells, ch), f32), terms, jnp.zeros((cells, LANES - dt_at - heads), f32)], axis=1)
    bias_lane = lax.broadcasted_iota(jnp.int32, (1, LANES), 1)
    bias = jnp.zeros((1, LANES), f32)
    for h in range(heads):
        bias = jnp.where(bias_lane == dt_at + h, bias_ref[h], bias)
    biased = terms + bias
    steps = mask * (jnp.maximum(biased, 0.0) + jnp.log1p(jnp.exp(-jnp.abs(biased))))
    w1.wait()
    per = LANES // ch
    for t in range(inner // LANES):
        vals = jnp.dot(x, win[:, t * LANES:(t + 1) * LANES], preferred_element_type=f32)
        vals = vals.astype(bf16).astype(f32) * mask
        for q in range(per):
            d = t * per + q
            h = (d * ch) // width
            moved = vals if q == 0 else pltpu.roll(vals, LANES - q * ch, 1)
            dts = steps if h == 0 else pltpu.roll(steps, LANES - h, 1)
            chunk = jnp.where(lane < ch, moved, jnp.where(lane < dt_at, terms, dts))
            send[d] = chunk.astype(bf16)

    beside = jnp.where(my_row > 0, 1, 0) + jnp.where(my_row < n_row - 1, 1, 0)
    pl.semaphore_wait(barrier, n_col - 1 + beside)

    def forth(g, o, landing):
        start, size = groups[g]
        part = pl.ds(start * SUB, size * SUB)
        return pltpu.make_async_remote_copy(
            src_ref=send.at[lax.rem(me + o, n_col), part], dst_ref=recv.at[landing, part],
            send_sem=s_sem.at[g, o], recv_sem=r_sem.at[g, o],
            device_id={"col": lax.rem(me + o, n_col)}, device_id_type=MESH)

    def back(g, o, landing):
        start, size = groups[g]
        part = pl.ds(start * SUB // 2, size * SUB // 2)
        return pltpu.make_async_remote_copy(
            src_ref=ysend.at[lax.rem(me + o, n_col), part], dst_ref=yrecv.at[landing, part],
            send_sem=ys_sem.at[g, o], recv_sem=yr_sem.at[g, o],
            device_id={"col": lax.rem(me + o, n_col)}, device_id_type=MESH)

    for g in range(len(groups)):
        for o in range(1, n_col):
            forth(g, o, me).start()
    own = pltpu.make_async_copy(send.at[me], recv.at[me], l_sem.at[0])
    own.start()

    w2.wait()
    for t in range(inner // LANES):
        z = jnp.dot(x, win[:, inner + t * LANES:inner + (t + 1) * LANES], preferred_element_type=f32)
        z = z.astype(bf16).astype(f32)
        zs[:, t * LANES:(t + 1) * LANES] = z * jax.nn.sigmoid(z)
    state[...] = jnp.zeros_like(state)
    own.wait()

    rate_x, rate_y, skip = ratex_ref[head], ratey_ref[head], skip_ref[head]
    down = lax.broadcasted_iota(jnp.int32, (jp, jp), 0)
    along = lax.broadcasted_iota(jnp.int32, (jp, jp), 1)
    tri = (along <= down).astype(bf16)
    cell_lane = lax.broadcasted_iota(jnp.int32, (jp, LANES), 1)

    def scan_rows(m, total):
        decays = []
        for k in range(2):
            both = recv[:, pl.ds(pl.multiple_of(m * 32 + k * 16, 16), 16), :].astype(f32)
            for p in range(2):
                i = 4 * m + 2 * k + p
                here = both[:, p * SUB:(p + 1) * SUB, :].reshape(jp, LANES)
                sums = jnp.dot(tri, here.astype(bf16), preferred_element_type=f32)
                sum_col = sums[:, dt_at:dt_at + 1]
                turned = jnp.where(cell_lane == dt_at + 1, sum_col, here).T
                tsc[i] = turned
                gap = turned[dt_at + 1:dt_at + 2, :] - sum_col
                decays.append(jnp.exp(jnp.where(down <= along, -rate_x * gap, -1e30)).astype(bf16))
                total = total + turned[dt_at:dt_at + 1, :]
                fade[i] = turned[ch + n_state:dt_at, :] * jnp.exp(-rate_y * total)
        for cb in range(blocks):
            now = state[cb]
            for r in range(4):
                i = 4 * m + r
                v = tsc[i, cb * block:(cb + 1) * block, :]
                b = tsc[i, ch:ch + n_state, :]
                c = tsc[i, ch + n_state:ch + 2 * n_state, :]
                dt = tsc[i, dt_at:dt_at + 1, :]
                source = (b[:, None, :] * (v * dt)[None, :, :]).reshape(n_state * block, jp)
                hx = jnp.dot(source.astype(bf16), decays[r], preferred_element_type=f32)
                now = jnp.exp(-rate_y * dt) * now + hx
                y = jnp.sum(c[:, None, :] * now.reshape(n_state, block, jp), axis=0) + skip * v
                ysc[i, cb * block:(cb + 1) * block, :] = y
            state[cb] = now
        return total

    def give_back(m, _):
        parts = []
        for k in range(2):
            pair = [ysc[4 * m + 2 * k], ysc[4 * m + 2 * k + 1]]
            if 2 * ch < LANES:
                pair.append(jnp.zeros((LANES - 2 * ch, jp), f32))
            parts.append(jnp.concatenate(pair, axis=0).T.reshape(n_col, SUB, LANES))
        ysend[:, pl.ds(pl.multiple_of(m * 16, 16), 16), :] = jnp.concatenate(parts, axis=1).astype(bf16)
        return 0

    def return_group(g):
        start, size = groups[g]
        lax.fori_loop(start // 4, (start + size) // 4, give_back, 0)
        for o in range(1, n_col):
            back(g, o, me).start()

    total = jnp.zeros((1, jp), f32)
    for g in range(len(groups)):
        start, size = groups[g]
        for o in range(1, n_col):
            forth(g, o, lax.rem(me + n_col - o, n_col)).wait_recv()
        total = lax.fori_loop(start // 4, (start + size) // 4, scan_rows, total)

        @pl.when(my_row == 0)
        def _():
            return_group(g)

    def pass_down(cb, to):
        return pltpu.make_async_remote_copy(
            src_ref=state.at[cb], dst_ref=carry.at[cb],
            send_sem=cs_sem.at[cb], recv_sem=cr_sem.at[cb],
            device_id={"row": to}, device_id_type=MESH)

    @pl.when(my_row == 0)
    def _():
        for cb in range(blocks):
            pass_down(cb, my_row + 1).start()

    @pl.when(my_row > 0)
    def _():
        for cb in range(blocks):
            pass_down(cb, my_row - 1).wait_recv()
            if n_row > 2:
                @pl.when(my_row < n_row - 1)
                def _():
                    state[cb] = state[cb] + jnp.exp(-rate_y * total) * carry[cb]
                    pass_down(cb, my_row + 1).start()

        def correct(m, _):
            for cb in range(blocks):
                held = carry[cb].reshape(n_state, block, jp)
                for r in range(4):
                    i = 4 * m + r
                    more = jnp.sum(fade[i][:, None, :] * held, axis=0)
                    ysc[i, cb * block:(cb + 1) * block, :] = ysc[i, cb * block:(cb + 1) * block, :] + more
            return 0

        for g in range(len(groups)):
            start, size = groups[g]
            lax.fori_loop(start // 4, (start + size) // 4, correct, 0)
            return_group(g)

    own_y = pltpu.make_async_copy(ysend.at[me], yrecv.at[me], l_sem.at[1])
    own_y.start()
    w3.wait()
    own_y.wait()

    @pl.when(my_row < n_row - 1)
    def _():
        for cb in range(blocks):
            pass_down(cb, my_row + 1).wait_send()

    for g in range(len(groups)):
        for o in range(1, n_col):
            forth(g, o, me).wait_send()
            back(g, o, lax.rem(me + n_col - o, n_col)).wait()

    half_lane = lax.broadcasted_iota(jnp.int32, (cells // 2, LANES), 1)
    squares = jnp.zeros((cells, 1), f32)
    for t in range(inner // LANES):
        parts = []
        for p in range(2):
            tile = None
            for q in range(per):
                piece = yrecv[t * per + q].astype(f32)
                shift = ((q - p) * ch) % LANES
                if shift:
                    piece = pltpu.roll(piece, shift, 1)
                tile = piece if tile is None else jnp.where(half_lane < q * ch, tile, piece)
            parts.append(tile.reshape(rows // 2, 1, SUB, LANES))
        y = jnp.concatenate(parts, axis=1).reshape(cells, LANES)
        z = zs[:, t * LANES:(t + 1) * LANES]
        g = y * z
        squares = squares + jnp.sum(g * g, axis=1, keepdims=True)
        yfull[:, t * LANES:(t + 1) * LANES] = g
    scale = lax.rsqrt(squares / inner + norm_eps)
    normed = (yfull[...] * scale * gain_ref[...]).astype(bf16)
    mixed = jnp.dot(normed, wout[...], preferred_element_type=f32) * mask
    out_ref[...] = mixed.reshape(rows, SUB, mixed.shape[1])[:, :cols, :].astype(bf16)


def per_device(slide, tissue, w_in, w_bcd, dt_bias, rate_x, rate_y, d_skip, norm_gain, w_out):
    rows, cols, model = slide.shape
    inner, heads = w_out.shape[0], dt_bias.shape[0]
    n_state = (w_bcd.shape[1] - heads) // 2
    width = inner // heads
    n_col, n_row = lax.axis_size("col"), lax.axis_size("row")
    ch = inner // n_col
    block = min(ch, 16)
    jp, cells = n_col * SUB, rows * SUB
    assert cols <= SUB and n_row > 1 and rows <= LANES and rows % 4 == 0 and 2 * ch <= LANES and width % ch == 0
    assert ch + 2 * n_state + heads <= LANES and ch % block == 0
    units = rows // 4
    splits = min(4, units)
    edges = [4 * ((units * g + splits - 1) // splits) for g in range(splits + 1)]
    groups = tuple((lo, hi - lo) for lo, hi in zip(edges[:-1], edges[1:]))
    vmem = pl.BlockSpec(memory_space=pltpu.VMEM)
    smem = pl.BlockSpec(memory_space=pltpu.SMEM)
    hbm = pl.BlockSpec(memory_space=pl.ANY)
    blocks = ch // block
    dims = (n_row, n_col, rows, cols, inner, heads, width, n_state, block, groups)
    dma = pltpu.SemaphoreType.DMA
    return pl.pallas_call(
        functools.partial(kernel, dims),
        out_shape=jax.ShapeDtypeStruct((rows, cols, model), bf16),
        in_specs=[vmem] * 4 + [smem] * 4 + [hbm] * 2,
        out_specs=vmem,
        scratch_shapes=[
            pltpu.VMEM(w_in.shape, bf16),
            pltpu.VMEM(w_out.shape, bf16),
            pltpu.VMEM((n_col, cells, LANES), bf16),
            pltpu.VMEM((n_col, cells, LANES), bf16),
            pltpu.VMEM((cells, inner), f32),
            pltpu.VMEM((rows, LANES, jp), f32),
            pltpu.VMEM((rows, n_state, jp), f32),
            pltpu.VMEM((rows, ch, jp), f32),
            pltpu.VMEM((blocks, n_state * block, jp), f32),
            pltpu.VMEM((blocks, n_state * block, jp), f32),
            pltpu.VMEM((n_col, cells // 2, LANES), bf16),
            pltpu.VMEM((n_col, cells // 2, LANES), bf16),
            pltpu.VMEM((cells, inner), f32),
            dma((3,)), *[dma((splits, n_col))] * 4,
            dma((blocks,)), dma((blocks,)), dma((2,)),
        ],
        compiler_params=pltpu.CompilerParams(
            collective_id=0, has_side_effects=True, vmem_limit_bytes=60 * 1024 * 1024),
        cost_estimate=pl.CostEstimate(flops=4 * 10**9, bytes_accessed=8 * 10**6, transcendentals=10**6),
    )(slide, tissue.T, w_bcd.T, norm_gain.reshape(1, inner), dt_bias, rate_x, rate_y, d_skip, w_in, w_out)


def solution(mesh):
    grid = P(("slides", "row"), "col")
    return jax.shard_map(
        per_device,
        mesh=mesh,
        in_specs=(P(("slides", "row"), "col", None), grid) + (P(),) * 8,
        out_specs=P(("slides", "row"), "col", None),
        check_vma=False,
    )
```
